32 devices in a mesh: grp: 2 (over y), wave: 4 (over z), lat: 4 (over x, core).
Axes of the slice: x: 2, y: 2, z: 4, core: 2. Of those that a mesh axis runs over, the one named last changes fastest.
Arguments:
- fourier: bfloat16 [5120, 8192], P(('grp', 'lat', 'wave')), parts along dimension 0, may hold values from -6 to 6
- row_points: int32 [2560], P(('lat', 'wave')), may hold values from 20 to 5260, as said below
- owner_order: int32 [16], replicated, may hold values from 0 to 15, each once
- gauss_weight: float32 [2560], P('lat'), may hold values from 0.5 to 2
- table: bfloat16 [16, 2560, 1280], P('wave', 'lat'), may hold values from -0.125 to 0.125
Outputs:
- spectral: float32 [2560, 8192], P(('grp', 'lat'), 'wave'), parts along dimension 0
The draws below stay inside these ranges and needn't reach their ends.
There are 2 independent parts, one for each index of `grp`. The reference program is written for one: setup_inputs(seed, part) draws one part's arguments, and reference() takes and returns one part's arrays. A program takes and returns all parts, laid end to end along the dimension named above; an argument that names none is the same for every part. Nothing has to cross between parts.
Inputs may be any that keep to these rules, and one draw needn't show every extreme that they name: `row_points`: row lengths of an octahedral reduced grid, 20 + 4 min(j, 2559 - j) points, plus 4 times a per-row extra of 0 to 31; the first row has no extra and row 1279 the most.
All inputs are finite; a program needn't handle non-finite values.
Results may differ from the reference program's by a relative error of at most 0.0029.
Values may be sent and summed in bfloat16 or wider, within the bound.
No kernel may reach another device: no remote copies, remote signals or barrier semaphores. Data moves between devices by JAX's collectives and lax.ppermute only.
A program may use at most 128 MiB of HBM per device.

```python
import math
import jax
import jax.numpy as jnp
from jax import lax

NLAT = 2560
NDEG = 1280
FIELDS = 256
MW = 16


def draw_row_points(key, part):
    key = jax.random.fold_in(key, 11)
    latitude = jnp.arange(NLAT, dtype=jnp.int32)
    rank_row = jnp.minimum(latitude, NLAT - 1 - latitude)
    extras = jax.random.randint(key, (NLAT,), 0, 32, dtype=jnp.int32)
    extras = jnp.where(latitude == 0, 0, extras)
    extras = jnp.where(latitude == NLAT // 2 - 1, 31, extras)
    return (20 + 4 * rank_row + 4 * extras).astype(jnp.int32)


def block_levels(own_key, dims, shards, low, top_value):
    def one(axis_at, blocks):
        draws = jax.random.uniform(jax.random.fold_in(jax.random.fold_in(own_key, 6), axis_at), (blocks,), jnp.float32, low / len(shards), top_value / len(shards))
        return jnp.repeat(jnp.exp(draws), dims[axis_at] // blocks).reshape((-1,) + (1,) * (len(dims) - axis_at - 1))

    loudness = one(*shards[0])
    for cut in shards[1:]:
        loudness = loudness * one(*cut)
    return loudness


def normal_values(stream_key, shape, deviation, reach, shards=(), held_as=jnp.bfloat16):
    gain = block_levels(stream_key, shape, shards, -0.22, 0.18) if shards else 1.0
    values = jax.random.normal(stream_key, shape, jnp.float32) * deviation * gain
    return jnp.minimum(jnp.maximum(values, -reach), reach).astype(held_as)


def setup_inputs(seed: int = 0, part: int = 0) -> dict:
    arg_keys = jax.random.split(jax.random.key(seed), 6)
    own_keys = jax.random.split(jax.random.fold_in(arg_keys[5], part), 6)
    fourier = normal_values(own_keys[0], (NLAT, MW * 2 * FIELDS), 1.0, 6.0, ((0, 16),))
    row_points = draw_row_points(jax.random.fold_in(arg_keys[5], 71), part)
    owner_order = jax.random.permutation(arg_keys[2], MW).astype(jnp.int32)
    gauss_weight = jnp.clip(jnp.exp(math.log(2.0) - 1.3862944 * jax.random.uniform(arg_keys[3], (NLAT,), jnp.float32) ** block_levels(arg_keys[3], (NLAT,), ((0, 4),), -0.2, 0.2)), 0.5, 2.0)
    table = normal_values(arg_keys[4], (MW, NLAT, NDEG), NLAT ** -0.5, 0.125, ((0, 4), (1, 4)))
    return dict(fourier=fourier, row_points=row_points, owner_order=owner_order, gauss_weight=gauss_weight, table=table)


def one_slot(operands):
    return lax.dot_general(operands[0], operands[1], (((0,), (0,)), ((), ())), preferred_element_type=jnp.float32)


def reference(fourier, row_points, owner_order, gauss_weight, table):
    slot_total = owner_order.shape[0]
    stride = NDEG // slot_total
    columns = fourier.shape[1] // slot_total
    wave_numbers = jnp.arange(slot_total, dtype=jnp.int32) * stride
    kept_mask = wave_numbers[None, :] < (row_points // 2)[:, None]
    spread = fourier.reshape(NLAT, slot_total, columns)
    spread = jnp.where(kept_mask[:, :, None], spread, jnp.zeros((), jnp.bfloat16))
    ordered = jnp.take(spread, owner_order, axis=1)
    weighted = (gauss_weight[:, None, None] * ordered.astype(jnp.float32)).astype(jnp.bfloat16)
    band_total = lax.map(one_slot, (table, jnp.transpose(weighted, (1, 0, 2))))
    band_total = jnp.transpose(band_total, (1, 0, 2))
    degree = jnp.arange(NDEG, dtype=jnp.int32)
    slot_wave = owner_order.astype(jnp.int32) * stride
    alive_mask = degree[:, None] >= slot_wave[None, :]
    spectral = jnp.where(alive_mask[:, :, None], band_total, jnp.zeros((), band_total.dtype))
    return spectral.reshape(NDEG, slot_total * columns)
```

```python
import functools

import jax
import jax.numpy as jnp
from jax import lax
from jax.experimental import pallas as pl
from jax.experimental.pallas import tpu as pltpu
from jax.sharding import PartitionSpec as P

WHOLE = pl.BlockSpec(memory_space=pltpu.VMEM)
SCALARS = pl.BlockSpec(memory_space=pltpu.SMEM)
PARAMS = pltpu.CompilerParams(vmem_limit_bytes=48 * 2**20)
SMALL = pl.CostEstimate(flops=1, transcendentals=0, bytes_accessed=1)
WINDOW = 3
CUTS = ((0, 0, 4), (1, 0, 4), (2, 0, 4), (3, 0, 3), (3, 3, 1))


def plain(fourier, row_points, owner_order, gauss_weight, table):
    slot_total = owner_order.shape[0]
    own_slots, band_count, degrees = table.shape
    stride = degrees // slot_total
    local_rows = fourier.shape[0]
    columns = fourier.shape[1] // slot_total
    wave_numbers = jnp.arange(slot_total, dtype=jnp.int32) * stride
    kept_mask = wave_numbers[None, :] < (row_points // 2)[:, None]
    spread = fourier.reshape(local_rows, slot_total, columns)
    spread = jnp.where(kept_mask[:, :, None], spread, jnp.zeros((), jnp.bfloat16))
    ordered = jnp.take(spread, owner_order, axis=1).reshape(local_rows, slot_total * columns)
    band_rows = lax.all_to_all(ordered, "wave", split_axis=1, concat_axis=0, tiled=True)
    weighted = (gauss_weight[:, None] * band_rows.astype(jnp.float32)).astype(jnp.bfloat16)
    weighted = weighted.reshape(band_count, own_slots, columns)
    share = degrees // lax.axis_size("lat")
    product = jnp.einsum("sjn,jsc->nsc", table, weighted, preferred_element_type=jnp.float32)
    totals = lax.psum_scatter(
        product.reshape(degrees, own_slots * columns), "lat", scatter_dimension=0, tiled=True
    )
    first_degree = lax.axis_index("lat") * share
    degree = first_degree + jnp.arange(share, dtype=jnp.int32)
    slot_wave = (
        lax.dynamic_slice_in_dim(owner_order, lax.axis_index("wave") * own_slots, own_slots)
        * stride
    )
    alive_mask = degree[:, None] >= slot_wave[None, :]
    shaped = totals.reshape(share, own_slots, columns)
    result = jnp.where(alive_mask[:, :, None], shaped, jnp.zeros((), jnp.float32))
    return result.reshape(share, own_slots * columns)


def exchange(value, axis, step):
    size = lax.axis_size(axis)
    with jax.named_scope(f"{axis}_{step}"):
        return lax.ppermute(value, axis, [(i, i ^ step) for i in range(size)])


def after(value, *earlier):
    return lax.optimization_barrier((value, *earlier))[0]


def prepare_body(stride, own_slots, chunks, owner_hbm, gauss_hbm, points_hbm, source, *refs):
    count = 4 * len(chunks)
    results, landed = refs[:count], refs[count : 2 * count]
    owner_ref, gauss_ref, points_ref, sems = refs[2 * count :]
    rows = points_ref.shape[0]
    band = gauss_ref.shape[0]
    columns = source.shape[1] // owner_ref.shape[0]
    wave = lax.axis_index("wave")

    copies = [
        pltpu.make_async_copy(gauss_hbm, gauss_ref, sems.at[count]),
        pltpu.make_async_copy(points_hbm, points_ref, sems.at[count + 1]),
    ]
    owners = pltpu.make_async_copy(owner_hbm, owner_ref, sems.at[count + 2])
    for copy in (owners, *copies):
        copy.start()
    owners.wait()
    kinds = []
    for at, (slot, offset, width) in enumerate(chunks):
        for step in range(4):
            kind = owner_ref[(wave ^ step) * own_slots + slot]
            start = pl.multiple_of(kind * columns + offset, 128)
            kinds.append(kind)
            copies.append(
                pltpu.make_async_copy(
                    source.at[:, pl.ds(start, width)],
                    landed[4 * at + step],
                    sems.at[4 * at + step],
                )
            )
    for copy in copies[2:]:
        copy.start()
    copies[0].wait()
    copies[1].wait()
    row = lax.broadcasted_iota(jnp.int32, (rows, band), 0)
    lane = lax.broadcasted_iota(jnp.int32, (rows, band), 1)
    weight = jnp.sum(
        jnp.where(lane == row + wave * rows, gauss_ref[...][None, :], 0.0), axis=1, keepdims=True
    )
    row = lax.broadcasted_iota(jnp.int32, (rows, rows), 0)
    lane = lax.broadcasted_iota(jnp.int32, (rows, rows), 1)
    points = jnp.sum(
        jnp.where(lane == row, points_ref[...].astype(jnp.float32)[None, :], 0.0),
        axis=1,
        keepdims=True,
    )
    for at in range(count):
        copies[2 + at].wait()
        kept = points >= (2 * kinds[at] * stride + 2).astype(jnp.float32)
        value = jnp.where(kept, landed[at][...].astype(jnp.float32) * weight, 0.0)
        results[at][...] = value.astype(jnp.bfloat16)


def prepare(fourier, row_points, owner_order, gauss_weight, own_slots, stride, chunks):
    rows = fourier.shape[0]
    blocks = [(rows, width) for _, _, width in chunks for _ in range(4)]
    hbm = pl.BlockSpec(memory_space=pltpu.HBM)
    outs = pl.pallas_call(
        functools.partial(prepare_body, stride, own_slots, chunks),
        in_specs=[hbm] * 4,
        out_specs=[WHOLE] * len(blocks),
        out_shape=[jax.ShapeDtypeStruct(block, jnp.bfloat16) for block in blocks],
        scratch_shapes=[pltpu.VMEM(block, jnp.bfloat16) for block in blocks]
        + [
            pltpu.SMEM(owner_order.shape, jnp.int32),
            pltpu.VMEM(gauss_weight.shape, jnp.float32),
            pltpu.VMEM(row_points.shape, jnp.int32),
            pltpu.SemaphoreType.DMA((len(blocks) + 3,)),
        ],
        compiler_params=PARAMS,
        cost_estimate=SMALL,
        name="prepare",
    )(
        *[
            pltpu.with_memory_space_constraint(array, pltpu.HBM)
            for array in (owner_order, gauss_weight, row_points, fourier)
        ],
    )
    return [list(outs[4 * at : 4 * at + 4]) for at in range(len(chunks))]


def turn_body(rows, stride, owner_ref, table_ref, limit_ref, *outs):
    wave = lax.axis_index("wave")
    own_slots = len(outs)
    for slot, out in enumerate(outs):
        limit_ref[slot] = jnp.full(
            limit_ref.shape[1:], owner_ref[wave * own_slots + slot] * stride, jnp.int32
        )
        for step in range(4):
            start = pl.multiple_of((wave ^ step) * rows, 16)
            out[:, step * rows : (step + 1) * rows] = table_ref[slot, pl.ds(start, rows), :].T


def turn(owner_order, table, rows, stride, columns):
    own_slots, band, degrees = table.shape
    return pl.pallas_call(
        functools.partial(turn_body, rows, stride),
        in_specs=[SCALARS, WHOLE],
        out_specs=[WHOLE] * (1 + own_slots),
        out_shape=[jax.ShapeDtypeStruct((own_slots, 8, columns), jnp.int32)]
        + [jax.ShapeDtypeStruct((degrees, band), table.dtype)] * own_slots,
        compiler_params=PARAMS,
        cost_estimate=SMALL,
        name="turn",
    )(owner_order, table)


def multiply_body(other, table_ref, own, one, two, three, out_ref):
    share = out_ref.shape[1]
    core = lax.axis_index("lat") & 1
    rows = jnp.concatenate([own[...], one[...], two[...], three[...]], axis=0)
    for half in range(2):
        start = pl.multiple_of((2 * half + (1 - core if other else core)) * share, 16)
        out_ref[half] = jnp.dot(
            table_ref[pl.ds(start, share), :], rows, preferred_element_type=jnp.float32
        ).astype(out_ref.dtype)


def multiply(turned, pieces, other):
    width = pieces[0].shape[1]
    share = turned.shape[0] // 4
    return pl.pallas_call(
        functools.partial(multiply_body, other),
        in_specs=[WHOLE] * 5,
        out_specs=WHOLE,
        out_shape=jax.ShapeDtypeStruct(
            (2, share, width), jnp.bfloat16 if other else jnp.float32
        ),
        compiler_params=PARAMS,
        cost_estimate=SMALL,
        name="multiply_other" if other else "multiply_own",
    )(turned, *pieces)


def combine_body(keep_ref, got_ref, send_ref):
    near = 1 - (lax.axis_index("lat") >> 1)
    send_ref[...] = (keep_ref[near] + got_ref[near].astype(jnp.float32)).astype(jnp.bfloat16)


def combine(keep, got):
    return pl.pallas_call(
        combine_body,
        in_specs=[WHOLE] * 2,
        out_specs=WHOLE,
        out_shape=jax.ShapeDtypeStruct(keep.shape[1:], jnp.bfloat16),
        compiler_params=PARAMS,
        cost_estimate=SMALL,
        name="combine",
    )(keep, got)


def finish_body(slot, start, limit_ref, keep_ref, near_ref, far_ref, *refs):
    out_ref, total_ref, sem = refs[-3:]
    share, width = total_ref.shape
    lat = lax.axis_index("lat")
    far = lat >> 1
    degree = lat * share + lax.broadcasted_iota(jnp.int32, (share, width), 0)
    total = keep_ref[far] + near_ref[far].astype(jnp.float32) + far_ref[...].astype(jnp.float32)
    total_ref[...] = jnp.where(degree >= limit_ref[slot, 0:1, :width], total, 0.0)
    copy = pltpu.make_async_copy(total_ref, out_ref.at[:, start : start + width], sem)
    copy.start()
    copy.wait()


def finish(limits, keep, near, far, before, chunk):
    _, share, width = keep.shape
    own_slots, _, columns = limits.shape
    slot, offset, _ = chunk
    old = [] if before is None else [before]
    hbm = pl.BlockSpec(memory_space=pltpu.HBM)
    return pl.pallas_call(
        functools.partial(finish_body, slot, slot * columns + offset),
        in_specs=[WHOLE] * 4 + [hbm] * len(old),
        out_specs=hbm,
        out_shape=pltpu.HBM((share, own_slots * columns), jnp.float32),
        input_output_aliases={4: 0} if old else {},
        scratch_shapes=[pltpu.VMEM((share, width), jnp.float32), pltpu.SemaphoreType.DMA],
        compiler_params=PARAMS,
        cost_estimate=SMALL,
        name="finish",
    )(limits, keep, near, far, *old)


def piped(fourier, row_points, owner_order, gauss_weight, table):
    slot_total = owner_order.shape[0]
    own_slots, _, degrees = table.shape
    stride = degrees // slot_total
    columns = fourier.shape[1] // slot_total
    chunks = [
        (slot, first * columns // 4, parts * columns // 4) for slot, first, parts in CUTS
    ]
    count = len(chunks)
    scalars = (fourier, row_points, owner_order, gauss_weight, own_slots, stride)
    pieces = prepare(*scalars, chunks[:1])
    arrived = [{0: piece[0]} for piece in pieces]
    queue = [(0, 2), (0, 3)]
    for at, step in queue + [(0, 1)]:
        arrived[at][step] = exchange(pieces[at][step], "wave", step)
    pieces += prepare(*scalars, chunks[1:])
    arrived += [{0: piece[0]} for piece in pieces[1:]]
    queue += [(at, step) for at in range(1, count) for step in (2, 3)]

    def send(place, *earlier):
        if place < len(queue):
            at, step = queue[place]
            if place >= WINDOW:
                was, by = queue[place - WINDOW]
                earlier = (*earlier, arrived[was][by])
            arrived[at][step] = exchange(after(pieces[at][step], *earlier), "wave", step)

    for place in range(2, WINDOW):
        send(place)
    limits, *turned = turn(
        after(owner_order, pieces[1][0]), table, fourier.shape[0], stride, columns
    )
    token = limits
    totals = pending = None
    for at, chunk in enumerate(chunks):
        if pending is not None:
            token = totals = finish(limits, *pending, totals, chunks[at - 1])
        for place in (2 * at + WINDOW, 2 * at + 1 + WINDOW):
            send(place, token)
        if at + 1 < count:
            arrived[at + 1][1] = exchange(
                after(pieces[at + 1][1], token, arrived[at][1]), "wave", 1
            )
        got = [arrived[at][step] for step in range(4)]
        got[0] = after(got[0], token, *got[1:])
        other = multiply(turned[chunk[0]], got, True)
        near = exchange(other, "lat", 1)
        got[0] = after(got[0], other)
        keep = multiply(turned[chunk[0]], got, False)
        token = sent = combine(keep, near)
        pending = (keep, near, exchange(sent, "lat", 2))
    return finish(limits, *pending, totals, chunks[-1])


def solution(mesh):
    in_specs = (
        P(("grp", "lat", "wave"), None),
        P(("lat", "wave")),
        P(),
        P("lat"),
        P("wave", "lat", None),
    )
    out_specs = P(("grp", "lat"), "wave")

    def per_device(fourier, row_points, owner_order, gauss_weight, table):
        columns = fourier.shape[1] // owner_order.shape[0]
        four = mesh.shape["wave"] == 4 and mesh.shape["lat"] == 4
        whole = (
            table.shape[0] == 4
            and fourier.shape[0] % 16 == 0
            and (table.shape[2] // 4) % 16 == 0
            and columns % 512 == 0
        )
        body = piped if four and whole else plain
        return body(fourier, row_points, owner_order, gauss_weight, table)

    return jax.shard_map(
        per_device, mesh=mesh, in_specs=in_specs, out_specs=out_specs, check_vma=False
    )
```

```python
import functools

import jax
import jax.numpy as jnp
from jax import lax
from jax.experimental import pallas as pl
from jax.experimental.pallas import tpu as pltpu
from jax.sharding import PartitionSpec as P

WHOLE = pl.BlockSpec(memory_space=pltpu.VMEM)
SCALARS = pl.BlockSpec(memory_space=pltpu.SMEM)
PARAMS = pltpu.CompilerParams(vmem_limit_bytes=48 * 2**20)
LARGE = pl.CostEstimate(flops=20_000_000_000, transcendentals=0, bytes_accessed=1)
SMALL = pl.CostEstimate(flops=1, transcendentals=0, bytes_accessed=1)
WINDOW = 6
EARLY = 2
STEPS = (2, 3, 1)
CUTS = (4, 8, 12, 14)


def plain(fourier, row_points, owner_order, gauss_weight, table):
    slot_total = owner_order.shape[0]
    own_slots, band_count, degrees = table.shape
    stride = degrees // slot_total
    local_rows = fourier.shape[0]
    columns = fourier.shape[1] // slot_total
    wave_numbers = jnp.arange(slot_total, dtype=jnp.int32) * stride
    kept_mask = wave_numbers[None, :] < (row_points // 2)[:, None]
    spread = fourier.reshape(local_rows, slot_total, columns)
    spread = jnp.where(kept_mask[:, :, None], spread, jnp.zeros((), jnp.bfloat16))
    ordered = jnp.take(spread, owner_order, axis=1).reshape(local_rows, slot_total * columns)
    band_rows = lax.all_to_all(ordered, "wave", split_axis=1, concat_axis=0, tiled=True)
    weighted = (gauss_weight[:, None] * band_rows.astype(jnp.float32)).astype(jnp.bfloat16)
    weighted = weighted.reshape(band_count, own_slots, columns)
    share = degrees // lax.axis_size("lat")
    product = jnp.einsum("sjn,jsc->nsc", table, weighted, preferred_element_type=jnp.float32)
    totals = lax.psum_scatter(
        product.reshape(degrees, own_slots * columns), "lat", scatter_dimension=0, tiled=True
    )
    first_degree = lax.axis_index("lat") * share
    degree = first_degree + jnp.arange(share, dtype=jnp.int32)
    slot_wave = (
        lax.dynamic_slice_in_dim(owner_order, lax.axis_index("wave") * own_slots, own_slots)
        * stride
    )
    alive_mask = degree[:, None] >= slot_wave[None, :]
    shaped = totals.reshape(share, own_slots, columns)
    result = jnp.where(alive_mask[:, :, None], shaped, jnp.zeros((), jnp.float32))
    return result.reshape(share, own_slots * columns)


def exchange(value, axis, step):
    size = lax.axis_size(axis)
    with jax.named_scope(f"{axis}_{step}"):
        return lax.ppermute(value, axis, [(i, i ^ step) for i in range(size)])


class Held(dict):
    def tie(self, *names):
        values = lax.optimization_barrier([self[name] for name in names])
        self.update(zip(names, values))


def units(first, last, columns):
    found = []
    for slot in range(first // columns, (last - 1) // columns + 1):
        start, stop = max(first, slot * columns), min(last, (slot + 1) * columns)
        found.append((slot, start - slot * columns, stop - start, start - first))
    return found


def prepare_body(stride, own_slots, chunks, masks, owner_hbm, gauss_hbm, points_hbm, source, *refs):
    count = 4 * len(chunks)
    results, landed = refs[:count], refs[count + masks : 2 * count + masks]
    owner_ref, gauss_ref, points_ref, sems = refs[2 * count + masks :]
    rows = points_ref.shape[0]
    band = gauss_ref.shape[0]
    columns = source.shape[1] // owner_ref.shape[0]
    wave = lax.axis_index("wave")

    small = [
        pltpu.make_async_copy(owner_hbm, owner_ref, sems.at[0]),
        pltpu.make_async_copy(gauss_hbm, gauss_ref, sems.at[1]),
        pltpu.make_async_copy(points_hbm, points_ref, sems.at[2]),
    ]
    for copy in small:
        copy.start()
    small[0].wait()
    blocks = []
    for at, (first, last) in enumerate(chunks):
        for step in STEPS + (0,):
            for slot, offset, width, place in units(first, last, columns):
                kind = owner_ref[(wave ^ step) * own_slots + slot]
                start = pl.multiple_of(kind * columns + offset, 128)
                into = (4 * at + step, place, place + width)
                copy = pltpu.make_async_copy(
                    source.at[:, pl.ds(start, width)],
                    landed[into[0]].at[:, place : place + width],
                    sems.at[3 + len(blocks)],
                )
                copy.start()
                blocks.append((copy, kind, *into))
    small[1].wait()
    small[2].wait()
    row = lax.broadcasted_iota(jnp.int32, (rows, band), 0)
    lane = lax.broadcasted_iota(jnp.int32, (rows, band), 1)
    weight = jnp.sum(
        jnp.where(lane == row + wave * rows, gauss_ref[...][None, :], 0.0), axis=1, keepdims=True
    )
    row = lax.broadcasted_iota(jnp.int32, (rows, rows), 0)
    lane = lax.broadcasted_iota(jnp.int32, (rows, rows), 1)
    points = jnp.sum(
        jnp.where(lane == row, points_ref[...].astype(jnp.float32)[None, :], 0.0),
        axis=1,
        keepdims=True,
    )
    if masks:
        limit_ref = refs[count]
        for slot in range(own_slots):
            limit_ref[:, slot * columns : (slot + 1) * columns] = jnp.full(
                (limit_ref.shape[0], columns), owner_ref[wave * own_slots + slot] * stride, jnp.int32
            )
    for copy, kind, at, start, stop in blocks:
        copy.wait()
        kept = points >= (2 * kind * stride + 2).astype(jnp.float32)
        value = jnp.where(kept, landed[at][:, start:stop].astype(jnp.float32) * weight, 0.0)
        results[at][:, start:stop] = value.astype(jnp.bfloat16)


def prepare(fourier, row_points, owner_order, gauss_weight, own_slots, stride, chunks, masks):
    rows = fourier.shape[0]
    columns = fourier.shape[1] // owner_order.shape[0]
    blocks = [(rows, last - first) for first, last in chunks for _ in range(4)]
    copies = 4 * sum(len(units(first, last, columns)) for first, last in chunks)
    limits = [jax.ShapeDtypeStruct((8, own_slots * columns), jnp.int32)] * masks
    outs = pl.pallas_call(
        functools.partial(prepare_body, stride, own_slots, chunks, masks),
        in_specs=[pl.BlockSpec(memory_space=pltpu.HBM)] * 4,
        out_specs=[WHOLE] * (len(blocks) + masks),
        out_shape=[jax.ShapeDtypeStruct(block, jnp.bfloat16) for block in blocks] + limits,
        scratch_shapes=[pltpu.VMEM(block, jnp.bfloat16) for block in blocks]
        + [
            pltpu.SMEM(owner_order.shape, jnp.int32),
            pltpu.VMEM(gauss_weight.shape, jnp.float32),
            pltpu.VMEM(row_points.shape, jnp.int32),
            pltpu.SemaphoreType.DMA((3 + copies,)),
        ],
        compiler_params=PARAMS,
        cost_estimate=SMALL,
        name="prepare",
    )(
        *[
            pltpu.with_memory_space_constraint(array, pltpu.HBM)
            for array in (owner_order, gauss_weight, row_points, fourier)
        ],
    )
    return outs


def turn_body(slot, rows, table_hbm, out_ref, table_ref, sem):
    wave = lax.axis_index("wave")
    copy = pltpu.make_async_copy(table_hbm.at[slot], table_ref, sem)
    copy.start()
    copy.wait()
    for step in range(4):
        start = pl.multiple_of((wave ^ step) * rows, 16)
        out_ref[:, step * rows : (step + 1) * rows] = table_ref[pl.ds(start, rows), :].T


def turn(table, slot, rows):
    _, band, degrees = table.shape
    return pl.pallas_call(
        functools.partial(turn_body, slot, rows),
        in_specs=[pl.BlockSpec(memory_space=pltpu.HBM)],
        out_specs=WHOLE,
        out_shape=jax.ShapeDtypeStruct((degrees, band), table.dtype),
        scratch_shapes=[pltpu.VMEM((band, degrees), table.dtype), pltpu.SemaphoreType.DMA],
        compiler_params=PARAMS,
        cost_estimate=SMALL,
        name="turn",
    )(pltpu.with_memory_space_constraint(table, pltpu.HBM))


def multiply_body(other, parts, *refs):
    tables, (own, one, two, three, out_ref) = refs[:-5], refs[-5:]
    share = out_ref.shape[1]
    core = lax.axis_index("lat") & 1
    for table_ref, (_, _, width, place) in zip(tables, parts):
        rows = jnp.concatenate(
            [piece[:, place : place + width] for piece in (own, one, two, three)], axis=0
        )
        for half in range(2):
            start = pl.multiple_of((2 * half + (1 - core if other else core)) * share, 16)
            out_ref[half, :, place : place + width] = jnp.dot(
                table_ref[pl.ds(start, share), :], rows, preferred_element_type=jnp.float32
            ).astype(out_ref.dtype)


def multiply(tables, parts, pieces, other):
    width = pieces[0].shape[1]
    share = tables[0].shape[0] // 4
    return pl.pallas_call(
        functools.partial(multiply_body, other, parts),
        in_specs=[WHOLE] * (len(tables) + 4),
        out_specs=WHOLE,
        out_shape=jax.ShapeDtypeStruct(
            (2, share, width), jnp.bfloat16 if other else jnp.float32
        ),
        compiler_params=PARAMS,
        cost_estimate=SMALL if other else LARGE,
        name="multiply_other" if other else "multiply_own",
    )(*tables, *pieces)


def combine_body(keep_ref, got_ref, send_ref):
    near = 1 - (lax.axis_index("lat") >> 1)
    send_ref[...] = (keep_ref[near] + got_ref[near].astype(jnp.float32)).astype(jnp.bfloat16)


def combine(keep, got):
    return pl.pallas_call(
        combine_body,
        in_specs=[WHOLE] * 2,
        out_specs=WHOLE,
        out_shape=jax.ShapeDtypeStruct(keep.shape[1:], jnp.bfloat16),
        compiler_params=PARAMS,
        cost_estimate=SMALL,
        name="combine",
    )(keep, got)


def finish_body(first, limit_ref, keep_ref, near_ref, far_ref, *refs):
    out_ref, total_ref, sem = refs[-3:]
    share, width = total_ref.shape
    lat = lax.axis_index("lat")
    far = lat >> 1
    degree = lat * share + lax.broadcasted_iota(jnp.int32, (share, width), 0)
    total = keep_ref[far] + near_ref[far].astype(jnp.float32) + far_ref[...].astype(jnp.float32)
    total_ref[...] = jnp.where(degree >= limit_ref[0:1, first : first + width], total, 0.0)
    copy = pltpu.make_async_copy(total_ref, out_ref.at[:, first : first + width], sem)
    copy.start()
    copy.wait()


def finish(limits, keep, near, far, before, first):
    _, share, width = keep.shape
    old = [] if before is None else [before]
    hbm = pl.BlockSpec(memory_space=pltpu.HBM)
    return pl.pallas_call(
        functools.partial(finish_body, first),
        in_specs=[WHOLE] * 4 + [hbm] * len(old),
        out_specs=hbm,
        out_shape=pltpu.HBM((share, limits.shape[1]), jnp.float32),
        input_output_aliases={4: 0} if old else {},
        scratch_shapes=[pltpu.VMEM((share, width), jnp.float32), pltpu.SemaphoreType.DMA],
        compiler_params=PARAMS,
        cost_estimate=SMALL,
        name="finish",
    )(limits, keep, near, far, *old)


def piped(fourier, row_points, owner_order, gauss_weight, table):
    slot_total = owner_order.shape[0]
    own_slots, _, degrees = table.shape
    stride = degrees // slot_total
    columns = fourier.shape[1] // slot_total
    grain = own_slots * columns // 16
    chunks = [(first * grain, last * grain) for first, last in zip((0,) + CUTS, CUTS + (16,))]
    count = len(chunks)
    scalars = (fourier, row_points, owner_order, gauss_weight, own_slots, stride)
    held = Held(table=table)
    queue = [(at, step) for at in range(count) for step in STEPS]

    def ready(first, last):
        masks = int(last == count)
        outs = prepare(*scalars, chunks[first:last], masks)
        for at in range(first, last):
            for step in range(4):
                name = "piece" if step else "row"
                held[name, at, step] = outs[4 * (at - first) + step]
        if masks:
            held["limits"] = outs[-1]

    def send(place):
        at, step = queue[place]
        if place >= WINDOW:
            held.tie(("piece", at, step), ("row", *queue[place - WINDOW]))
        held["row", at, step] = exchange(held["piece", at, step], "wave", step)

    def sums(at, other):
        parts = units(*chunks[at], columns)
        rows = [held["row", at, step] for step in range(4)]
        return multiply([held["turned", part[0]] for part in parts], parts, rows, other)

    def multiply_other(at):
        held["other", at] = sums(at, True)

    def pass_core(at):
        held["near", at] = exchange(held["other", at], "lat", 1)

    def multiply_own(at):
        held["keep", at] = sums(at, False)

    def join(at):
        held["sent", at] = combine(held["keep", at], held["near", at])

    def pass_on(at):
        held["far", at] = exchange(held["sent", at], "lat", 2)

    def close(at):
        held["out"] = finish(
            held["limits"],
            held["keep", at],
            held["near", at],
            held["far", at],
            held.get("out"),
            chunks[at][0],
        )

    ready(0, 1)
    for place in range(3):
        send(place)
    ready(1, count)

    def turn_slots(first, last):
        for slot in range(first, last):
            held["turned", slot] = turn(held["table"], slot, fourier.shape[0])

    held.tie("table", ("piece", 1, STEPS[0]))
    turn_slots(0, EARLY)
    held.tie(*[("piece", 1, step) for step in STEPS[1:]], "table")
    for place in range(3, 6):
        send(place)
    for at in range(count):
        if at >= 2:
            held.tie(("row", at, 0), "out")
        multiply_other(at)
        pass_core(at)
        held.tie(("row", at, 0), ("other", at))
        multiply_own(at)
        join(at)
        if at + 2 < count:
            held.tie(*[("piece", at + 2, step) for step in STEPS], ("sent", at))
        pass_on(at)
        if at == 0:
            held.tie("table", ("sent", at))
            turn_slots(EARLY, own_slots)
        for place in range(3 * at + 6, min(3 * at + 9, len(queue))):
            send(place)
        if at >= 1:
            held.tie(("far", at - 1), ("sent", at))
            close(at - 1)
    close(count - 1)
    return held["out"]


def solution(mesh):
    in_specs = (
        P(("grp", "lat", "wave"), None),
        P(("lat", "wave")),
        P(),
        P("lat"),
        P("wave", "lat", None),
    )
    out_specs = P(("grp", "lat"), "wave")

    def per_device(fourier, row_points, owner_order, gauss_weight, table):
        columns = fourier.shape[1] // owner_order.shape[0]
        four = mesh.shape["wave"] == 4 and mesh.shape["lat"] == 4
        whole = (
            table.shape[0] == 4
            and fourier.shape[0] % 16 == 0
            and (table.shape[2] // 4) % 16 == 0
            and columns % 512 == 0
        )
        body = piped if four and whole else plain
        return body(fourier, row_points, owner_order, gauss_weight, table)

    return jax.shard_map(
        per_device, mesh=mesh, in_specs=in_specs, out_specs=out_specs, check_vma=False
    )
```

```python
import functools

import jax
import jax.numpy as jnp
from jax import lax
from jax.experimental import pallas as pl
from jax.experimental.pallas import tpu as pltpu
from jax.sharding import PartitionSpec as P

WHOLE = pl.BlockSpec(memory_space=pltpu.VMEM)
SCALARS = pl.BlockSpec(memory_space=pltpu.SMEM)
PARAMS = pltpu.CompilerParams(vmem_limit_bytes=48 * 2**20)
LARGE = pl.CostEstimate(flops=1, transcendentals=0, bytes_accessed=1)
HUGE = pl.CostEstimate(flops=20000000000, transcendentals=0, bytes_accessed=1)
SMALL = pl.CostEstimate(flops=1, transcendentals=0, bytes_accessed=1)
WINDOW = 6
EARLY = 2
PINS = ('sent', 'none', 'none', 'none')
OUTS = 1
SEQ = (1, 1, 1, 1, 1)
CLOSE = 1
STEPS = (2, 3, 1)
CUTS = (4, 8, 12)


def plain(fourier, row_points, owner_order, gauss_weight, table):
    slot_total = owner_order.shape[0]
    own_slots, band_count, degrees = table.shape
    stride = degrees // slot_total
    local_rows = fourier.shape[0]
    columns = fourier.shape[1] // slot_total
    wave_numbers = jnp.arange(slot_total, dtype=jnp.int32) * stride
    kept_mask = wave_numbers[None, :] < (row_points // 2)[:, None]
    spread = fourier.reshape(local_rows, slot_total, columns)
    spread = jnp.where(kept_mask[:, :, None], spread, jnp.zeros((), jnp.bfloat16))
    ordered = jnp.take(spread, owner_order, axis=1).reshape(local_rows, slot_total * columns)
    band_rows = lax.all_to_all(ordered, "wave", split_axis=1, concat_axis=0, tiled=True)
    weighted = (gauss_weight[:, None] * band_rows.astype(jnp.float32)).astype(jnp.bfloat16)
    weighted = weighted.reshape(band_count, own_slots, columns)
    share = degrees // lax.axis_size("lat")
    product = jnp.einsum("sjn,jsc->nsc", table, weighted, preferred_element_type=jnp.float32)
    totals = lax.psum_scatter(
        product.reshape(degrees, own_slots * columns), "lat", scatter_dimension=0, tiled=True
    )
    first_degree = lax.axis_index("lat") * share
    degree = first_degree + jnp.arange(share, dtype=jnp.int32)
    slot_wave = (
        lax.dynamic_slice_in_dim(owner_order, lax.axis_index("wave") * own_slots, own_slots)
        * stride
    )
    alive_mask = degree[:, None] >= slot_wave[None, :]
    shaped = totals.reshape(share, own_slots, columns)
    result = jnp.where(alive_mask[:, :, None], shaped, jnp.zeros((), jnp.float32))
    return result.reshape(share, own_slots * columns)


def exchange(value, axis, step):
    size = lax.axis_size(axis)
    with jax.named_scope(f"{axis}_{step}"):
        return lax.ppermute(value, axis, [(i, i ^ step) for i in range(size)])


class Held(dict):
    def tie(self, *names):
        values = lax.optimization_barrier([self[name] for name in names])
        self.update(zip(names, values))


def units(first, last, columns):
    found = []
    for slot in range(first // columns, (last - 1) // columns + 1):
        start, stop = max(first, slot * columns), min(last, (slot + 1) * columns)
        found.append((slot, start - slot * columns, stop - start, start - first))
    return found


def prepare_body(stride, own_slots, chunks, masks, owner_hbm, gauss_hbm, points_hbm, source, *refs):
    count = 4 * len(chunks)
    results, landed = refs[:count], refs[count + masks : 2 * count + masks]
    owner_ref, gauss_ref, points_ref, sems = refs[2 * count + masks :]
    rows = points_ref.shape[0]
    band = gauss_ref.shape[0]
    columns = source.shape[1] // owner_ref.shape[0]
    wave = lax.axis_index("wave")

    small = [
        pltpu.make_async_copy(owner_hbm, owner_ref, sems.at[0]),
        pltpu.make_async_copy(gauss_hbm, gauss_ref, sems.at[1]),
        pltpu.make_async_copy(points_hbm, points_ref, sems.at[2]),
    ]
    for copy in small:
        copy.start()
    small[0].wait()
    blocks = []
    for at, (first, last) in enumerate(chunks):
        for step in STEPS + (0,):
            for slot, offset, width, place in units(first, last, columns):
                kind = owner_ref[(wave ^ step) * own_slots + slot]
                start = pl.multiple_of(kind * columns + offset, 128)
                into = (4 * at + step, place, place + width)
                copy = pltpu.make_async_copy(
                    source.at[:, pl.ds(start, width)],
                    landed[into[0]].at[:, place : place + width],
                    sems.at[3 + len(blocks)],
                )
                copy.start()
                blocks.append((copy, kind, *into))
    small[1].wait()
    small[2].wait()
    row = lax.broadcasted_iota(jnp.int32, (rows, band), 0)
    lane = lax.broadcasted_iota(jnp.int32, (rows, band), 1)
    weight = jnp.sum(
        jnp.where(lane == row + wave * rows, gauss_ref[...][None, :], 0.0), axis=1, keepdims=True
    )
    row = lax.broadcasted_iota(jnp.int32, (rows, rows), 0)
    lane = lax.broadcasted_iota(jnp.int32, (rows, rows), 1)
    points = jnp.sum(
        jnp.where(lane == row, points_ref[...].astype(jnp.float32)[None, :], 0.0),
        axis=1,
        keepdims=True,
    )
    if masks:
        limit_ref = refs[count]
        for slot in range(own_slots):
            limit_ref[:, slot * columns : (slot + 1) * columns] = jnp.full(
                (limit_ref.shape[0], columns), owner_ref[wave * own_slots + slot] * stride, jnp.int32
            )
    for copy, kind, at, start, stop in blocks:
        copy.wait()
        kept = points >= (2 * kind * stride + 2).astype(jnp.float32)
        value = jnp.where(kept, landed[at][:, start:stop].astype(jnp.float32) * weight, 0.0)
        results[at][:, start:stop] = value.astype(jnp.bfloat16)


def prepare(fourier, row_points, owner_order, gauss_weight, own_slots, stride, chunks, masks):
    rows = fourier.shape[0]
    columns = fourier.shape[1] // owner_order.shape[0]
    blocks = [(rows, last - first) for first, last in chunks for _ in range(4)]
    copies = 4 * sum(len(units(first, last, columns)) for first, last in chunks)
    limits = [jax.ShapeDtypeStruct((8, own_slots * columns), jnp.int32)] * masks
    outs = pl.pallas_call(
        functools.partial(prepare_body, stride, own_slots, chunks, masks),
        in_specs=[pl.BlockSpec(memory_space=pltpu.HBM)] * 4,
        out_specs=[WHOLE] * (len(blocks) + masks),
        out_shape=[jax.ShapeDtypeStruct(block, jnp.bfloat16) for block in blocks] + limits,
        scratch_shapes=[pltpu.VMEM(block, jnp.bfloat16) for block in blocks]
        + [
            pltpu.SMEM(owner_order.shape, jnp.int32),
            pltpu.VMEM(gauss_weight.shape, jnp.float32),
            pltpu.VMEM(row_points.shape, jnp.int32),
            pltpu.SemaphoreType.DMA((3 + copies,)),
        ],
        compiler_params=PARAMS,
        cost_estimate=SMALL,
        name="prepare",
    )(
        *[
            pltpu.with_memory_space_constraint(array, pltpu.HBM)
            for array in (owner_order, gauss_weight, row_points, fourier)
        ],
    )
    return outs


def turn_body(slot, rows, table_hbm, out_ref, table_ref, sem):
    wave = lax.axis_index("wave")
    copy = pltpu.make_async_copy(table_hbm.at[slot], table_ref, sem)
    copy.start()
    copy.wait()
    for step in range(4):
        start = pl.multiple_of((wave ^ step) * rows, 16)
        out_ref[:, step * rows : (step + 1) * rows] = table_ref[pl.ds(start, rows), :].T


def turn(table, slot, rows):
    _, band, degrees = table.shape
    return pl.pallas_call(
        functools.partial(turn_body, slot, rows),
        in_specs=[pl.BlockSpec(memory_space=pltpu.HBM)],
        out_specs=WHOLE,
        out_shape=jax.ShapeDtypeStruct((degrees, band), table.dtype),
        scratch_shapes=[pltpu.VMEM((band, degrees), table.dtype), pltpu.SemaphoreType.DMA],
        compiler_params=PARAMS,
        cost_estimate=SMALL,
        name="turn",
    )(pltpu.with_memory_space_constraint(table, pltpu.HBM))


def multiply_body(other, parts, *refs):
    tables, (own, one, two, three, out_ref) = refs[:-5], refs[-5:]
    share = out_ref.shape[1]
    core = lax.axis_index("lat") & 1
    for table_ref, (_, _, width, place) in zip(tables, parts):
        rows = jnp.concatenate(
            [piece[:, place : place + width] for piece in (own, one, two, three)], axis=0
        )
        for half in range(2):
            start = pl.multiple_of((2 * half + (1 - core if other else core)) * share, 16)
            out_ref[half, :, place : place + width] = jnp.dot(
                table_ref[pl.ds(start, share), :], rows, preferred_element_type=jnp.float32
            ).astype(out_ref.dtype)


def multiply(tables, parts, pieces, other):
    width = pieces[0].shape[1]
    share = tables[0].shape[0] // 4
    return pl.pallas_call(
        functools.partial(multiply_body, other, parts),
        in_specs=[WHOLE] * (len(tables) + 4),
        out_specs=WHOLE,
        out_shape=jax.ShapeDtypeStruct(
            (2, share, width), jnp.bfloat16 if other else jnp.float32
        ),
        compiler_params=PARAMS,
        cost_estimate=LARGE if other else HUGE,
        name="multiply_other" if other else "multiply_own",
    )(*tables, *pieces)


def combine_body(keep_ref, got_ref, send_ref):
    near = 1 - (lax.axis_index("lat") >> 1)
    send_ref[...] = (keep_ref[near] + got_ref[near].astype(jnp.float32)).astype(jnp.bfloat16)


def combine(keep, got):
    return pl.pallas_call(
        combine_body,
        in_specs=[WHOLE] * 2,
        out_specs=WHOLE,
        out_shape=jax.ShapeDtypeStruct(keep.shape[1:], jnp.bfloat16),
        compiler_params=PARAMS,
        cost_estimate=SMALL,
        name="combine",
    )(keep, got)


def finish_body(first, limit_ref, keep_ref, near_ref, far_ref, *refs):
    out_ref, total_ref, sem = refs[-3:]
    share, width = total_ref.shape
    lat = lax.axis_index("lat")
    far = lat >> 1
    degree = lat * share + lax.broadcasted_iota(jnp.int32, (share, width), 0)
    total = keep_ref[far] + near_ref[far].astype(jnp.float32) + far_ref[...].astype(jnp.float32)
    total_ref[...] = jnp.where(degree >= limit_ref[0:1, first : first + width], total, 0.0)
    copy = pltpu.make_async_copy(total_ref, out_ref.at[:, first : first + width], sem)
    copy.start()
    copy.wait()


def finish(limits, keep, near, far, before, first):
    _, share, width = keep.shape
    old = [] if before is None else [before]
    hbm = pl.BlockSpec(memory_space=pltpu.HBM)
    return pl.pallas_call(
        functools.partial(finish_body, first),
        in_specs=[WHOLE] * 4 + [hbm] * len(old),
        out_specs=hbm,
        out_shape=pltpu.HBM((share, limits.shape[1]), jnp.float32),
        input_output_aliases={4: 0} if old else {},
        scratch_shapes=[pltpu.VMEM((share, width), jnp.float32), pltpu.SemaphoreType.DMA],
        compiler_params=PARAMS,
        cost_estimate=SMALL,
        name="finish",
    )(limits, keep, near, far, *old)


def piped(fourier, row_points, owner_order, gauss_weight, table):
    slot_total = owner_order.shape[0]
    own_slots, _, degrees = table.shape
    stride = degrees // slot_total
    columns = fourier.shape[1] // slot_total
    grain = own_slots * columns // 16
    chunks = [(first * grain, last * grain) for first, last in zip((0,) + CUTS, CUTS + (16,))]
    count = len(chunks)
    scalars = (fourier, row_points, owner_order, gauss_weight, own_slots, stride)
    held = Held(table=table)
    queue = [(at, step) for at in range(count) for step in STEPS]

    def ready(first, last):
        masks = int(last == count)
        outs = prepare(*scalars, chunks[first:last], masks)
        for at in range(first, last):
            for step in range(4):
                name = "piece" if step else "row"
                held[name, at, step] = outs[4 * (at - first) + step]
        if masks:
            held["limits"] = outs[-1]

    def send(place):
        at, step = queue[place]
        if place >= WINDOW:
            held.tie(("piece", at, step), ("row", *queue[place - WINDOW]))
        held["row", at, step] = exchange(held["piece", at, step], "wave", step)

    def sums(at, other):
        parts = units(*chunks[at], columns)
        rows = [held["row", at, step] for step in range(4)]
        return multiply([held["turned", part[0]] for part in parts], parts, rows, other)

    def multiply_other(at):
        held["other", at] = sums(at, True)

    def pass_core(at):
        held["near", at] = exchange(held["other", at], "lat", 1)

    def multiply_own(at):
        held["keep", at] = sums(at, False)

    def join(at):
        held["sent", at] = combine(held["keep", at], held["near", at])

    def pass_on(at):
        held["far", at] = exchange(held["sent", at], "lat", 2)

    def close(at):
        held["out"] = finish(
            held["limits"],
            held["keep", at],
            held["near", at],
            held["far", at],
            held.get("out"),
            chunks[at][0],
        )

    ready(0, 1)
    for place in range(3):
        send(place)
    ready(1, count)

    def turn_slots(first, last):
        for slot in range(first, last):
            held["turned", slot] = turn(held["table"], slot, fourier.shape[0])

    held.tie("table", ("piece", 1, STEPS[0]))
    turn_slots(0, EARLY)
    held.tie(*[("piece", 1, step) for step in STEPS[1:]], "table")
    for place in range(3, 6):
        send(place)
    def hold(at, name):
        if at + 2 < count and PINS[at] == name:
            held.tie(*[("piece", at + 2, step) for step in STEPS], (name, at))

    for at in range(count):
        if at >= 2 and OUTS:
            held.tie(("row", at, 0), "out")
        if at >= 1 and SEQ[at - 1]:
            held.tie(("row", at, 0), ("sent", at - 1))
        multiply_other(at)
        hold(at, "other")
        pass_core(at)
        held.tie(("row", at, 0), ("other", at))
        multiply_own(at)
        hold(at, "keep")
        join(at)
        hold(at, "sent")
        pass_on(at)
        if at == 0:
            held.tie("table", ("sent", at))
            turn_slots(EARLY, own_slots)
        for place in range(3 * at + 6, min(3 * at + 9, len(queue))):
            send(place)
        if at >= CLOSE:
            held.tie(("far", at - CLOSE), ("sent", at))
            close(at - CLOSE)
    for at in range(count - CLOSE, count):
        close(at)
    return held["out"]


def solution(mesh):
    in_specs = (
        P(("grp", "lat", "wave"), None),
        P(("lat", "wave")),
        P(),
        P("lat"),
        P("wave", "lat", None),
    )
    out_specs = P(("grp", "lat"), "wave")

    def per_device(fourier, row_points, owner_order, gauss_weight, table):
        columns = fourier.shape[1] // owner_order.shape[0]
        four = mesh.shape["wave"] == 4 and mesh.shape["lat"] == 4
        whole = (
            table.shape[0] == 4
            and fourier.shape[0] % 16 == 0
            and (table.shape[2] // 4) % 16 == 0
            and columns % 512 == 0
        )
        body = piped if four and whole else plain
        return body(fourier, row_points, owner_order, gauss_weight, table)

    return jax.shard_map(
        per_device, mesh=mesh, in_specs=in_specs, out_specs=out_specs, check_vma=False
    )
```

```python
import functools

import jax
import jax.numpy as jnp
from jax import lax
from jax.experimental import pallas as pl
from jax.experimental.pallas import tpu as pltpu
from jax.sharding import PartitionSpec as P

WHOLE = pl.BlockSpec(memory_space=pltpu.VMEM)
SCALARS = pl.BlockSpec(memory_space=pltpu.SMEM)
PARAMS = pltpu.CompilerParams(vmem_limit_bytes=48 * 2**20)
LARGE = pl.CostEstimate(flops=1, transcendentals=0, bytes_accessed=1)
HUGE = pl.CostEstimate(flops=20000000000, transcendentals=0, bytes_accessed=1)
SMALL = pl.CostEstimate(flops=1, transcendentals=0, bytes_accessed=1)
WINDOW = 7
EARLY = 2
PINS = ('sent', 'none', 'sent', 'none')
OUTS = 1
SEQ = (1, 1, 1, 1, 1)
CLOSE = 1
STEPS = (2, 3, 1)
CUTS = (4, 8, 12)


def plain(fourier, row_points, owner_order, gauss_weight, table):
    slot_total = owner_order.shape[0]
    own_slots, band_count, degrees = table.shape
    stride = degrees // slot_total
    local_rows = fourier.shape[0]
    columns = fourier.shape[1] // slot_total
    wave_numbers = jnp.arange(slot_total, dtype=jnp.int32) * stride
    kept_mask = wave_numbers[None, :] < (row_points // 2)[:, None]
    spread = fourier.reshape(local_rows, slot_total, columns)
    spread = jnp.where(kept_mask[:, :, None], spread, jnp.zeros((), jnp.bfloat16))
    ordered = jnp.take(spread, owner_order, axis=1).reshape(local_rows, slot_total * columns)
    band_rows = lax.all_to_all(ordered, "wave", split_axis=1, concat_axis=0, tiled=True)
    weighted = (gauss_weight[:, None] * band_rows.astype(jnp.float32)).astype(jnp.bfloat16)
    weighted = weighted.reshape(band_count, own_slots, columns)
    share = degrees // lax.axis_size("lat")
    product = jnp.einsum("sjn,jsc->nsc", table, weighted, preferred_element_type=jnp.float32)
    totals = lax.psum_scatter(
        product.reshape(degrees, own_slots * columns), "lat", scatter_dimension=0, tiled=True
    )
    first_degree = lax.axis_index("lat") * share
    degree = first_degree + jnp.arange(share, dtype=jnp.int32)
    slot_wave = (
        lax.dynamic_slice_in_dim(owner_order, lax.axis_index("wave") * own_slots, own_slots)
        * stride
    )
    alive_mask = degree[:, None] >= slot_wave[None, :]
    shaped = totals.reshape(share, own_slots, columns)
    result = jnp.where(alive_mask[:, :, None], shaped, jnp.zeros((), jnp.float32))
    return result.reshape(share, own_slots * columns)


def exchange(value, axis, step):
    size = lax.axis_size(axis)
    with jax.named_scope(f"{axis}_{step}"):
        return lax.ppermute(value, axis, [(i, i ^ step) for i in range(size)])


class Held(dict):
    def tie(self, *names):
        values = lax.optimization_barrier([self[name] for name in names])
        self.update(zip(names, values))


def units(first, last, columns):
    found = []
    for slot in range(first // columns, (last - 1) // columns + 1):
        start, stop = max(first, slot * columns), min(last, (slot + 1) * columns)
        found.append((slot, start - slot * columns, stop - start, start - first))
    return found


def prepare_body(stride, own_slots, chunks, masks, owner_hbm, gauss_hbm, points_hbm, source, *refs):
    count = 4 * len(chunks)
    results, landed = refs[:count], refs[count + masks : 2 * count + masks]
    owner_ref, gauss_ref, points_ref, sems = refs[2 * count + masks :]
    rows = points_ref.shape[0]
    band = gauss_ref.shape[0]
    columns = source.shape[1] // owner_ref.shape[0]
    wave = lax.axis_index("wave")

    small = [
        pltpu.make_async_copy(owner_hbm, owner_ref, sems.at[0]),
        pltpu.make_async_copy(gauss_hbm, gauss_ref, sems.at[1]),
        pltpu.make_async_copy(points_hbm, points_ref, sems.at[2]),
    ]
    for copy in small:
        copy.start()
    small[0].wait()
    blocks = []
    for at, (first, last) in enumerate(chunks):
        for step in STEPS + (0,):
            for slot, offset, width, place in units(first, last, columns):
                kind = owner_ref[(wave ^ step) * own_slots + slot]
                start = pl.multiple_of(kind * columns + offset, 128)
                into = (4 * at + step, place, place + width)
                copy = pltpu.make_async_copy(
                    source.at[:, pl.ds(start, width)],
                    landed[into[0]].at[:, place : place + width],
                    sems.at[3 + len(blocks)],
                )
                copy.start()
                blocks.append((copy, kind, *into))
    small[1].wait()
    small[2].wait()
    row = lax.broadcasted_iota(jnp.int32, (rows, band), 0)
    lane = lax.broadcasted_iota(jnp.int32, (rows, band), 1)
    weight = jnp.sum(
        jnp.where(lane == row + wave * rows, gauss_ref[...][None, :], 0.0), axis=1, keepdims=True
    )
    row = lax.broadcasted_iota(jnp.int32, (rows, rows), 0)
    lane = lax.broadcasted_iota(jnp.int32, (rows, rows), 1)
    points = jnp.sum(
        jnp.where(lane == row, points_ref[...].astype(jnp.float32)[None, :], 0.0),
        axis=1,
        keepdims=True,
    )
    if masks:
        limit_ref = refs[count]
        for slot in range(own_slots):
            limit_ref[:, slot * columns : (slot + 1) * columns] = jnp.full(
                (limit_ref.shape[0], columns), owner_ref[wave * own_slots + slot] * stride, jnp.int32
            )
    for copy, kind, at, start, stop in blocks:
        copy.wait()
        kept = points >= (2 * kind * stride + 2).astype(jnp.float32)
        value = jnp.where(kept, landed[at][:, start:stop].astype(jnp.float32) * weight, 0.0)
        results[at][:, start:stop] = value.astype(jnp.bfloat16)


def prepare(fourier, row_points, owner_order, gauss_weight, own_slots, stride, chunks, masks):
    rows = fourier.shape[0]
    columns = fourier.shape[1] // owner_order.shape[0]
    blocks = [(rows, last - first) for first, last in chunks for _ in range(4)]
    copies = 4 * sum(len(units(first, last, columns)) for first, last in chunks)
    limits = [jax.ShapeDtypeStruct((8, own_slots * columns), jnp.int32)] * masks
    outs = pl.pallas_call(
        functools.partial(prepare_body, stride, own_slots, chunks, masks),
        in_specs=[pl.BlockSpec(memory_space=pltpu.HBM)] * 4,
        out_specs=[WHOLE] * (len(blocks) + masks),
        out_shape=[jax.ShapeDtypeStruct(block, jnp.bfloat16) for block in blocks] + limits,
        scratch_shapes=[pltpu.VMEM(block, jnp.bfloat16) for block in blocks]
        + [
            pltpu.SMEM(owner_order.shape, jnp.int32),
            pltpu.VMEM(gauss_weight.shape, jnp.float32),
            pltpu.VMEM(row_points.shape, jnp.int32),
            pltpu.SemaphoreType.DMA((3 + copies,)),
        ],
        compiler_params=PARAMS,
        cost_estimate=SMALL,
        name="prepare",
    )(
        *[
            pltpu.with_memory_space_constraint(array, pltpu.HBM)
            for array in (owner_order, gauss_weight, row_points, fourier)
        ],
    )
    return outs


def turn_body(slot, rows, table_hbm, out_ref, table_ref, sem):
    wave = lax.axis_index("wave")
    copy = pltpu.make_async_copy(table_hbm.at[slot], table_ref, sem)
    copy.start()
    copy.wait()
    for step in range(4):
        start = pl.multiple_of((wave ^ step) * rows, 16)
        out_ref[:, step * rows : (step + 1) * rows] = table_ref[pl.ds(start, rows), :].T


def turn(table, slot, rows):
    _, band, degrees = table.shape
    return pl.pallas_call(
        functools.partial(turn_body, slot, rows),
        in_specs=[pl.BlockSpec(memory_space=pltpu.HBM)],
        out_specs=WHOLE,
        out_shape=jax.ShapeDtypeStruct((degrees, band), table.dtype),
        scratch_shapes=[pltpu.VMEM((band, degrees), table.dtype), pltpu.SemaphoreType.DMA],
        compiler_params=PARAMS,
        cost_estimate=SMALL,
        name="turn",
    )(pltpu.with_memory_space_constraint(table, pltpu.HBM))


def multiply_body(other, parts, *refs):
    tables, (own, one, two, three, out_ref) = refs[:-5], refs[-5:]
    share = out_ref.shape[1]
    core = lax.axis_index("lat") & 1
    for table_ref, (_, _, width, place) in zip(tables, parts):
        rows = jnp.concatenate(
            [piece[:, place : place + width] for piece in (own, one, two, three)], axis=0
        )
        for half in range(2):
            start = pl.multiple_of((2 * half + (1 - core if other else core)) * share, 16)
            out_ref[half, :, place : place + width] = jnp.dot(
                table_ref[pl.ds(start, share), :], rows, preferred_element_type=jnp.float32
            ).astype(out_ref.dtype)


def multiply(tables, parts, pieces, other):
    width = pieces[0].shape[1]
    share = tables[0].shape[0] // 4
    return pl.pallas_call(
        functools.partial(multiply_body, other, parts),
        in_specs=[WHOLE] * (len(tables) + 4),
        out_specs=WHOLE,
        out_shape=jax.ShapeDtypeStruct(
            (2, share, width), jnp.bfloat16 if other else jnp.float32
        ),
        compiler_params=PARAMS,
        cost_estimate=LARGE if other else HUGE,
        name="multiply_other" if other else "multiply_own",
    )(*tables, *pieces)


def combine_body(keep_ref, got_ref, send_ref):
    near = 1 - (lax.axis_index("lat") >> 1)
    send_ref[...] = (keep_ref[near] + got_ref[near].astype(jnp.float32)).astype(jnp.bfloat16)


def combine(keep, got):
    return pl.pallas_call(
        combine_body,
        in_specs=[WHOLE] * 2,
        out_specs=WHOLE,
        out_shape=jax.ShapeDtypeStruct(keep.shape[1:], jnp.bfloat16),
        compiler_params=PARAMS,
        cost_estimate=SMALL,
        name="combine",
    )(keep, got)


def finish_body(first, limit_ref, keep_ref, near_ref, far_ref, *refs):
    out_ref, total_ref, sem = refs[-3:]
    share, width = total_ref.shape
    lat = lax.axis_index("lat")
    far = lat >> 1
    degree = lat * share + lax.broadcasted_iota(jnp.int32, (share, width), 0)
    total = keep_ref[far] + near_ref[far].astype(jnp.float32) + far_ref[...].astype(jnp.float32)
    total_ref[...] = jnp.where(degree >= limit_ref[0:1, first : first + width], total, 0.0)
    copy = pltpu.make_async_copy(total_ref, out_ref.at[:, first : first + width], sem)
    copy.start()
    copy.wait()


def finish(limits, keep, near, far, before, first):
    _, share, width = keep.shape
    old = [] if before is None else [before]
    hbm = pl.BlockSpec(memory_space=pltpu.HBM)
    return pl.pallas_call(
        functools.partial(finish_body, first),
        in_specs=[WHOLE] * 4 + [hbm] * len(old),
        out_specs=hbm,
        out_shape=pltpu.HBM((share, limits.shape[1]), jnp.float32),
        input_output_aliases={4: 0} if old else {},
        scratch_shapes=[pltpu.VMEM((share, width), jnp.float32), pltpu.SemaphoreType.DMA],
        compiler_params=PARAMS,
        cost_estimate=SMALL,
        name="finish",
    )(limits, keep, near, far, *old)


def piped(fourier, row_points, owner_order, gauss_weight, table):
    slot_total = owner_order.shape[0]
    own_slots, _, degrees = table.shape
    stride = degrees // slot_total
    columns = fourier.shape[1] // slot_total
    grain = own_slots * columns // 16
    chunks = [(first * grain, last * grain) for first, last in zip((0,) + CUTS, CUTS + (16,))]
    count = len(chunks)
    scalars = (fourier, row_points, owner_order, gauss_weight, own_slots, stride)
    held = Held(table=table)
    queue = [(at, step) for at in range(count) for step in STEPS]

    def ready(first, last):
        masks = int(last == count)
        outs = prepare(*scalars, chunks[first:last], masks)
        for at in range(first, last):
            for step in range(4):
                name = "piece" if step else "row"
                held[name, at, step] = outs[4 * (at - first) + step]
        if masks:
            held["limits"] = outs[-1]

    def send(place):
        at, step = queue[place]
        if place >= WINDOW:
            held.tie(("piece", at, step), ("row", *queue[place - WINDOW]))
        held["row", at, step] = exchange(held["piece", at, step], "wave", step)

    def sums(at, other):
        parts = units(*chunks[at], columns)
        rows = [held["row", at, step] for step in range(4)]
        return multiply([held["turned", part[0]] for part in parts], parts, rows, other)

    def multiply_other(at):
        held["other", at] = sums(at, True)

    def pass_core(at):
        held["near", at] = exchange(held["other", at], "lat", 1)

    def multiply_own(at):
        held["keep", at] = sums(at, False)

    def join(at):
        held["sent", at] = combine(held["keep", at], held["near", at])

    def pass_on(at):
        held["far", at] = exchange(held["sent", at], "lat", 2)

    def close(at):
        held["out"] = finish(
            held["limits"],
            held["keep", at],
            held["near", at],
            held["far", at],
            held.get("out"),
            chunks[at][0],
        )

    ready(0, 1)
    for place in range(3):
        send(place)
    ready(1, count)

    def turn_slots(first, last):
        for slot in range(first, last):
            held["turned", slot] = turn(held["table"], slot, fourier.shape[0])

    held.tie("table", ("piece", 1, STEPS[0]))
    turn_slots(0, EARLY)
    held.tie(*[("piece", 1, step) for step in STEPS[1:]], "table")
    for place in range(3, 6):
        send(place)
    def hold(at, name):
        if at + 2 < count and PINS[at] == name:
            held.tie(*[("piece", at + 2, step) for step in STEPS], (name, at))

    for at in range(count):
        if at >= 2 and OUTS:
            held.tie(("row", at, 0), "out")
        if at >= 1 and SEQ[at - 1]:
            held.tie(("row", at, 0), ("keep", at - 1), ("near", at - 1))
        multiply_other(at)
        hold(at, "other")
        pass_core(at)
        held.tie(("row", at, 0), ("other", at))
        multiply_own(at)
        hold(at, "keep")
        join(at)
        hold(at, "sent")
        pass_on(at)
        if at == 0:
            held.tie("table", ("sent", at))
            turn_slots(EARLY, own_slots)
        for place in range(3 * at + 6, min(3 * at + 9, len(queue))):
            send(place)
        if at >= CLOSE:
            held.tie(("far", at - CLOSE), ("sent", at))
            close(at - CLOSE)
    for at in range(count - CLOSE, count):
        close(at)
    return held["out"]


def solution(mesh):
    in_specs = (
        P(("grp", "lat", "wave"), None),
        P(("lat", "wave")),
        P(),
        P("lat"),
        P("wave", "lat", None),
    )
    out_specs = P(("grp", "lat"), "wave")

    def per_device(fourier, row_points, owner_order, gauss_weight, table):
        columns = fourier.shape[1] // owner_order.shape[0]
        four = mesh.shape["wave"] == 4 and mesh.shape["lat"] == 4
        whole = (
            table.shape[0] == 4
            and fourier.shape[0] % 16 == 0
            and (table.shape[2] // 4) % 16 == 0
            and columns % 512 == 0
        )
        body = piped if four and whole else plain
        return body(fourier, row_points, owner_order, gauss_weight, table)

    return jax.shard_map(
        per_device, mesh=mesh, in_specs=in_specs, out_specs=out_specs, check_vma=False
    )
```

```python
import functools

import jax
import jax.numpy as jnp
from jax import lax
from jax.experimental import pallas as pl
from jax.experimental.pallas import tpu as pltpu
from jax.sharding import PartitionSpec as P

WHOLE = pl.BlockSpec(memory_space=pltpu.VMEM)
SCALARS = pl.BlockSpec(memory_space=pltpu.SMEM)
PARAMS = pltpu.CompilerParams(vmem_limit_bytes=48 * 2**20)
LARGE = pl.CostEstimate(flops=1, transcendentals=0, bytes_accessed=1)
HUGE = pl.CostEstimate(flops=20000000000, transcendentals=0, bytes_accessed=1)
SMALL = pl.CostEstimate(flops=1, transcendentals=0, bytes_accessed=1)
WINDOW = 7
EARLY = 2
PINS = ('sent', 'none', 'sent', 'none')
OUTS = 1
SEQ = (1, 1, 1, 1, 1)
CLOSE = 1
STEPS = (2, 3, 1)
CUTS = (4, 8, 12)


def plain(fourier, row_points, owner_order, gauss_weight, table):
    slot_total = owner_order.shape[0]
    own_slots, band_count, degrees = table.shape
    stride = degrees // slot_total
    local_rows = fourier.shape[0]
    columns = fourier.shape[1] // slot_total
    wave_numbers = jnp.arange(slot_total, dtype=jnp.int32) * stride
    kept_mask = wave_numbers[None, :] < (row_points // 2)[:, None]
    spread = fourier.reshape(local_rows, slot_total, columns)
    spread = jnp.where(kept_mask[:, :, None], spread, jnp.zeros((), jnp.bfloat16))
    ordered = jnp.take(spread, owner_order, axis=1).reshape(local_rows, slot_total * columns)
    band_rows = lax.all_to_all(ordered, "wave", split_axis=1, concat_axis=0, tiled=True)
    weighted = (gauss_weight[:, None] * band_rows.astype(jnp.float32)).astype(jnp.bfloat16)
    weighted = weighted.reshape(band_count, own_slots, columns)
    share = degrees // lax.axis_size("lat")
    product = jnp.einsum("sjn,jsc->nsc", table, weighted, preferred_element_type=jnp.float32)
    totals = lax.psum_scatter(
        product.reshape(degrees, own_slots * columns), "lat", scatter_dimension=0, tiled=True
    )
    first_degree = lax.axis_index("lat") * share
    degree = first_degree + jnp.arange(share, dtype=jnp.int32)
    slot_wave = (
        lax.dynamic_slice_in_dim(owner_order, lax.axis_index("wave") * own_slots, own_slots)
        * stride
    )
    alive_mask = degree[:, None] >= slot_wave[None, :]
    shaped = totals.reshape(share, own_slots, columns)
    result = jnp.where(alive_mask[:, :, None], shaped, jnp.zeros((), jnp.float32))
    return result.reshape(share, own_slots * columns)


def exchange(value, axis, step):
    size = lax.axis_size(axis)
    with jax.named_scope(f"{axis}_{step}"):
        return lax.ppermute(value, axis, [(i, i ^ step) for i in range(size)])


class Held(dict):
    def tie(self, *names):
        values = lax.optimization_barrier([self[name] for name in names])
        self.update(zip(names, values))


def units(first, last, columns):
    found = []
    for slot in range(first // columns, (last - 1) // columns + 1):
        start, stop = max(first, slot * columns), min(last, (slot + 1) * columns)
        found.append((slot, start - slot * columns, stop - start, start - first))
    return found


def prepare_body(stride, own_slots, chunks, masks, owner_hbm, gauss_hbm, points_hbm, source, *refs):
    count = 4 * len(chunks)
    results, landed = refs[:count], refs[count + masks : 2 * count + masks]
    owner_ref, gauss_ref, points_ref, sems = refs[2 * count + masks :]
    rows = points_ref.shape[0]
    band = gauss_ref.shape[0]
    columns = source.shape[1] // owner_ref.shape[0]
    wave = lax.axis_index("wave")

    small = [
        pltpu.make_async_copy(owner_hbm, owner_ref, sems.at[0]),
        pltpu.make_async_copy(gauss_hbm, gauss_ref, sems.at[1]),
        pltpu.make_async_copy(points_hbm, points_ref, sems.at[2]),
    ]
    for copy in small:
        copy.start()
    small[0].wait()
    blocks = []
    for at, (first, last) in enumerate(chunks):
        for step in STEPS + (0,):
            for slot, offset, width, place in units(first, last, columns):
                kind = owner_ref[(wave ^ step) * own_slots + slot]
                start = pl.multiple_of(kind * columns + offset, 128)
                into = (4 * at + step, place, place + width)
                copy = pltpu.make_async_copy(
                    source.at[:, pl.ds(start, width)],
                    landed[into[0]].at[:, place : place + width],
                    sems.at[3 + len(blocks)],
                )
                copy.start()
                blocks.append((copy, kind, *into))
    small[1].wait()
    small[2].wait()
    row = lax.broadcasted_iota(jnp.int32, (rows, band), 0)
    lane = lax.broadcasted_iota(jnp.int32, (rows, band), 1)
    weight = jnp.sum(
        jnp.where(lane == row + wave * rows, gauss_ref[...][None, :], 0.0), axis=1, keepdims=True
    )
    row = lax.broadcasted_iota(jnp.int32, (rows, rows), 0)
    lane = lax.broadcasted_iota(jnp.int32, (rows, rows), 1)
    points = jnp.sum(
        jnp.where(lane == row, points_ref[...].astype(jnp.float32)[None, :], 0.0),
        axis=1,
        keepdims=True,
    )
    if masks:
        limit_ref = refs[count]
        for slot in range(own_slots):
            limit_ref[:, slot * columns : (slot + 1) * columns] = jnp.full(
                (limit_ref.shape[0], columns), owner_ref[wave * own_slots + slot] * stride, jnp.int32
            )
    for copy, kind, at, start, stop in blocks:
        copy.wait()
        kept = points >= (2 * kind * stride + 2).astype(jnp.float32)
        value = jnp.where(kept, landed[at][:, start:stop].astype(jnp.float32) * weight, 0.0)
        results[at][:, start:stop] = value.astype(jnp.bfloat16)


def prepare(fourier, row_points, owner_order, gauss_weight, own_slots, stride, chunks, masks):
    rows = fourier.shape[0]
    columns = fourier.shape[1] // owner_order.shape[0]
    blocks = [(rows, last - first) for first, last in chunks for _ in range(4)]
    copies = 4 * sum(len(units(first, last, columns)) for first, last in chunks)
    limits = [jax.ShapeDtypeStruct((8, own_slots * columns), jnp.int32)] * masks
    outs = pl.pallas_call(
        functools.partial(prepare_body, stride, own_slots, chunks, masks),
        in_specs=[pl.BlockSpec(memory_space=pltpu.HBM)] * 4,
        out_specs=[WHOLE] * (len(blocks) + masks),
        out_shape=[jax.ShapeDtypeStruct(block, jnp.bfloat16) for block in blocks] + limits,
        scratch_shapes=[pltpu.VMEM(block, jnp.bfloat16) for block in blocks]
        + [
            pltpu.SMEM(owner_order.shape, jnp.int32),
            pltpu.VMEM(gauss_weight.shape, jnp.float32),
            pltpu.VMEM(row_points.shape, jnp.int32),
            pltpu.SemaphoreType.DMA((3 + copies,)),
        ],
        compiler_params=PARAMS,
        cost_estimate=SMALL,
        name="prepare",
    )(
        *[
            pltpu.with_memory_space_constraint(array, pltpu.HBM)
            for array in (owner_order, gauss_weight, row_points, fourier)
        ],
    )
    return outs


def turn_body(slot, rows, table_hbm, out_ref, table_ref, sem):
    wave = lax.axis_index("wave")
    copy = pltpu.make_async_copy(table_hbm.at[slot], table_ref, sem)
    copy.start()
    copy.wait()
    for step in range(4):
        start = pl.multiple_of((wave ^ step) * rows, 16)
        out_ref[:, step * rows : (step + 1) * rows] = table_ref[pl.ds(start, rows), :].T


def turn(table, slot, rows):
    _, band, degrees = table.shape
    return pl.pallas_call(
        functools.partial(turn_body, slot, rows),
        in_specs=[pl.BlockSpec(memory_space=pltpu.HBM)],
        out_specs=WHOLE,
        out_shape=jax.ShapeDtypeStruct((degrees, band), table.dtype),
        scratch_shapes=[pltpu.VMEM((band, degrees), table.dtype), pltpu.SemaphoreType.DMA],
        compiler_params=PARAMS,
        cost_estimate=SMALL,
        name="turn",
    )(pltpu.with_memory_space_constraint(table, pltpu.HBM))


def multiply_body(other, parts, *refs):
    tables, (own, one, two, three, out_ref) = refs[:-5], refs[-5:]
    share = out_ref.shape[1]
    core = lax.axis_index("lat") & 1
    for table_ref, (_, _, width, place) in zip(tables, parts):
        rows = jnp.concatenate(
            [piece[:, place : place + width] for piece in (own, one, two, three)], axis=0
        )
        for half in range(2):
            start = pl.multiple_of((2 * half + (1 - core if other else core)) * share, 16)
            out_ref[half, :, place : place + width] = jnp.dot(
                table_ref[pl.ds(start, share), :], rows, preferred_element_type=jnp.float32
            ).astype(out_ref.dtype)


def multiply(tables, parts, pieces, other):
    width = pieces[0].shape[1]
    share = tables[0].shape[0] // 4
    return pl.pallas_call(
        functools.partial(multiply_body, other, parts),
        in_specs=[WHOLE] * (len(tables) + 4),
        out_specs=WHOLE,
        out_shape=jax.ShapeDtypeStruct(
            (2, share, width), jnp.bfloat16 if other else jnp.float32
        ),
        compiler_params=PARAMS,
        cost_estimate=LARGE if other else HUGE,
        name="multiply_other" if other else "multiply_own",
    )(*tables, *pieces)


def combine_body(keep_ref, got_ref, send_ref):
    near = 1 - (lax.axis_index("lat") >> 1)
    send_ref[...] = (keep_ref[near] + got_ref[near].astype(jnp.float32)).astype(jnp.bfloat16)


def combine(keep, got):
    return pl.pallas_call(
        combine_body,
        in_specs=[WHOLE] * 2,
        out_specs=WHOLE,
        out_shape=jax.ShapeDtypeStruct(keep.shape[1:], jnp.bfloat16),
        compiler_params=PARAMS,
        cost_estimate=SMALL,
        name="combine",
    )(keep, got)


def finish_body(first, limit_ref, keep_ref, near_ref, far_ref, *refs):
    out_ref, total_ref, sem = refs[-3:]
    share, width = total_ref.shape
    lat = lax.axis_index("lat")
    far = lat >> 1
    part = share // 4
    copies = []
    for at in range(4):
        rows = slice(at * part, (at + 1) * part)
        degree = lat * share + at * part + lax.broadcasted_iota(jnp.int32, (part, width), 0)
        total = keep_ref[far, rows, :] + near_ref[far, rows, :].astype(jnp.float32)
        total = total + far_ref[rows, :].astype(jnp.float32)
        total_ref[rows, :] = jnp.where(degree >= limit_ref[0:1, first : first + width], total, 0.0)
        copy = pltpu.make_async_copy(
            total_ref.at[rows, :], out_ref.at[rows, first : first + width], sem.at[at]
        )
        copy.start()
        copies.append(copy)
    for copy in copies:
        copy.wait()


def finish(limits, keep, near, far, before, first):
    _, share, width = keep.shape
    old = [] if before is None else [before]
    hbm = pl.BlockSpec(memory_space=pltpu.HBM)
    return pl.pallas_call(
        functools.partial(finish_body, first),
        in_specs=[WHOLE] * 4 + [hbm] * len(old),
        out_specs=hbm,
        out_shape=pltpu.HBM((share, limits.shape[1]), jnp.float32),
        input_output_aliases={4: 0} if old else {},
        scratch_shapes=[pltpu.VMEM((share, width), jnp.float32), pltpu.SemaphoreType.DMA((4,))],
        compiler_params=PARAMS,
        cost_estimate=SMALL,
        name="finish",
    )(limits, keep, near, far, *old)


def piped(fourier, row_points, owner_order, gauss_weight, table):
    slot_total = owner_order.shape[0]
    own_slots, _, degrees = table.shape
    stride = degrees // slot_total
    columns = fourier.shape[1] // slot_total
    grain = own_slots * columns // 16
    chunks = [(first * grain, last * grain) for first, last in zip((0,) + CUTS, CUTS + (16,))]
    count = len(chunks)
    scalars = (fourier, row_points, owner_order, gauss_weight, own_slots, stride)
    held = Held(table=table)
    queue = [(at, step) for at in range(count) for step in STEPS]

    def ready(first, last):
        masks = int(last == count)
        outs = prepare(*scalars, chunks[first:last], masks)
        for at in range(first, last):
            for step in range(4):
                name = "piece" if step else "row"
                held[name, at, step] = outs[4 * (at - first) + step]
        if masks:
            held["limits"] = outs[-1]

    def send(place):
        at, step = queue[place]
        if place >= WINDOW:
            held.tie(("piece", at, step), ("row", *queue[place - WINDOW]))
        held["row", at, step] = exchange(held["piece", at, step], "wave", step)

    def sums(at, other):
        parts = units(*chunks[at], columns)
        rows = [held["row", at, step] for step in range(4)]
        return multiply([held["turned", part[0]] for part in parts], parts, rows, other)

    def multiply_other(at):
        held["other", at] = sums(at, True)

    def pass_core(at):
        held["near", at] = exchange(held["other", at], "lat", 1)

    def multiply_own(at):
        held["keep", at] = sums(at, False)

    def join(at):
        held["sent", at] = combine(held["keep", at], held["near", at])

    def pass_on(at):
        held["far", at] = exchange(held["sent", at], "lat", 2)

    def close(at):
        held["out"] = finish(
            held["limits"],
            held["keep", at],
            held["near", at],
            held["far", at],
            held.get("out"),
            chunks[at][0],
        )

    ready(0, 1)
    for place in range(3):
        send(place)
    ready(1, count)

    def turn_slots(first, last):
        for slot in range(first, last):
            held["turned", slot] = turn(held["table"], slot, fourier.shape[0])

    held.tie("table", ("piece", 1, STEPS[0]))
    turn_slots(0, EARLY)
    held.tie(*[("piece", 1, step) for step in STEPS[1:]], "table")
    for place in range(3, 6):
        send(place)
    def hold(at, name):
        if at + 2 < count and PINS[at] == name:
            held.tie(*[("piece", at + 2, step) for step in STEPS], (name, at))

    for at in range(count):
        if at >= 2 and OUTS:
            held.tie(("row", at, 0), "out")
        if at >= 1 and SEQ[at - 1]:
            held.tie(("row", at, 0), ("keep", at - 1), ("near", at - 1))
        multiply_other(at)
        hold(at, "other")
        pass_core(at)
        held.tie(("row", at, 0), ("other", at))
        multiply_own(at)
        hold(at, "keep")
        join(at)
        hold(at, "sent")
        pass_on(at)
        if at == 0:
            held.tie("table", ("sent", at))
            turn_slots(EARLY, own_slots)
        for place in range(3 * at + 6, min(3 * at + 9, len(queue))):
            send(place)
        if at >= CLOSE:
            held.tie(("far", at - CLOSE), ("sent", at))
            close(at - CLOSE)
    for at in range(count - CLOSE, count):
        close(at)
    return held["out"]


def solution(mesh):
    in_specs = (
        P(("grp", "lat", "wave"), None),
        P(("lat", "wave")),
        P(),
        P("lat"),
        P("wave", "lat", None),
    )
    out_specs = P(("grp", "lat"), "wave")

    def per_device(fourier, row_points, owner_order, gauss_weight, table):
        columns = fourier.shape[1] // owner_order.shape[0]
        four = mesh.shape["wave"] == 4 and mesh.shape["lat"] == 4
        whole = (
            table.shape[0] == 4
            and fourier.shape[0] % 16 == 0
            and (table.shape[2] // 4) % 16 == 0
            and columns % 512 == 0
        )
        body = piped if four and whole else plain
        return body(fourier, row_points, owner_order, gauss_weight, table)

    return jax.shard_map(
        per_device, mesh=mesh, in_specs=in_specs, out_specs=out_specs, check_vma=False
    )
```
